32 devices in a mesh: branch: 2 (over core), group: 2 (over y), seq: 8 (over z, x).
Axes of the slice: x: 2, y: 2, z: 4, core: 2. Of those that a mesh axis runs over, the one named last changes fastest.
Arguments:
- query_rows: bfloat16 [2, 2560, 4096], P('branch', ('group', 'seq')), parts along dimension 1, may hold values from -10 to 10
- key_rows: bfloat16 [2, 2560, 4096], P('branch', ('group', 'seq')), parts along dimension 1, may hold values from -9 to 9
- value_rows: bfloat16 [2, 2560, 4096], P('branch', ('group', 'seq')), parts along dimension 1, may hold values from -80 to 80
- residual: bfloat16 [2560, 2560], P(('group', 'seq')), parts along dimension 0, may hold values from -6 to 6
- control_mask: int32 [2560], P(('group', 'seq')), parts along dimension 0, may hold values 0 or 1
- step_index: int32 [2], P('group'), parts along dimension 0, may hold values from 0 to 49
- step_gates: float32 [50, 2560], replicated, may hold values from 0.1 to 1.9
- out_weight: bfloat16 [2, 4096, 2560], P('branch', None, 'seq'), may hold values from -0.109375 to 0.109375
Outputs:
- block_out: bfloat16 [2, 2560, 2560], P('branch', ('group', 'seq')), parts along dimension 1
The draws below stay inside these ranges and needn't reach their ends.
There are 2 independent parts, one for each index of `group`. The reference program is written for one: setup_inputs(seed, part) draws one part's arguments, and reference() takes and returns one part's arrays. A program takes and returns all parts, laid end to end along the dimension named above; an argument that names none is the same for every part. Nothing has to cross between parts.
All inputs are finite; a program needn't handle non-finite values. No bound on the sum of `control_mask` on one device may be relied on, other than what follows from the above.
Results may differ from the reference program's by a relative error of at most 0.007.
Values may be sent and summed in bfloat16 or wider, within the bound.
No kernel may reach another device: no remote copies, remote signals or barrier semaphores. Data moves between devices by JAX's collectives and lax.ppermute only.
A program may use at most 128 MiB of HBM per device.

```python
import jax
import jax.numpy as jnp
from jax import lax

HEADS = 32
DH = 128
DW = 2560
STEPS = 50
HF = 4096
TOKENS = 1280


def base_field(key, shape):
    return jax.random.normal(key, shape, jnp.float32)


def draw_query_rows(key, part):
    drawn = jnp.clip(2.0 * base_field(jax.random.fold_in(key, 1), (2, TOKENS, HEADS, DH)), -9.0, 9.0)
    return drawn.reshape(2, TOKENS, HEADS * DH).astype(jnp.bfloat16)


def draw_key_rows(key, part):
    drawn = jnp.clip(base_field(jax.random.fold_in(key, 2), (2, TOKENS, HEADS, DH)), -9.0, 9.0)
    return drawn.reshape(2, TOKENS, HEADS * DH).astype(jnp.bfloat16)


def draw_value_rows(key, part):
    row_scale = 10.0 ** jax.random.uniform(jax.random.fold_in(key, 3), (2, TOKENS, 1), jnp.float32, 0.0, 1.0)
    noise = jnp.clip(base_field(jax.random.fold_in(key, 4), (2, TOKENS, HEADS * DH)), -6.0, 6.0)
    field = row_scale * noise
    return field.astype(jnp.bfloat16)


def place_ends(values, rng, least, high):
    longest = values.shape.index(max(values.shape))
    spots = []
    for shift in (0, 1):
        where = [jax.random.randint(jax.random.fold_in(rng, axis), (), 0, length) for axis, length in enumerate(values.shape)]
        where[longest] = (where[longest] + shift) % values.shape[longest]
        spots.append(tuple(where))
    return values.at[spots[0]].set(least).at[spots[1]].set(high)


def block_levels(rng, dims, split, least, high):
    def one(axis_at, blocks):
        heights = jax.random.uniform(jax.random.fold_in(jax.random.fold_in(rng, 6), axis_at), (blocks,), jnp.float32, least / len(split), high / len(split))
        return jnp.repeat(jnp.exp(heights), dims[axis_at] // blocks).reshape((-1,) + (1,) * (len(dims) - axis_at - 1))

    level = one(*split[0])
    for cut in split[1:]:
        level = level * one(*cut)
    return level


def centred(own_key, shape, spread, limit, cuts=(), held_as=jnp.bfloat16):
    array = jax.random.normal(own_key, shape, jnp.float32) * spread
    if len(cuts) > 0:
        array = block_levels(own_key, shape, cuts, -0.22, 0.18) * array
    return jnp.clip(array, min=-limit, max=limit).astype(held_as)


def setup_inputs(seed: int = 0, part: int = 0) -> dict:
    keys = jax.random.split(jax.random.key(seed), 9)
    part_splits = jax.random.split(jax.random.fold_in(keys[8], part), 9)
    query_rows = draw_query_rows(jax.random.fold_in(jax.random.fold_in(keys[8], part), 71), part)
    key_rows = draw_key_rows(jax.random.fold_in(jax.random.fold_in(keys[8], part), 71), part)
    value_rows = draw_value_rows(jax.random.fold_in(jax.random.fold_in(keys[8], part), 71), part)
    residual = centred(part_splits[3], (TOKENS, DW), 1.0, 6.0, ((0, 8),))
    control_mask = place_ends((jax.random.randint(part_splits[4], (TOKENS,), 0, 4) < 3).astype(jnp.int32), jax.random.fold_in(part_splits[4], 1), 0, 1)
    step_index = jax.random.randint(part_splits[5], (1,), 0, STEPS).astype(jnp.int32)
    step_gates = jnp.clip(1.0 + 0.18 * jax.random.normal(keys[6], (STEPS, DW), jnp.float32), 0.1, 1.9)
    out_weight = centred(keys[7], (2, HF, DW), (HF * 1024 // TOKENS) ** -0.5, 0.109375, ((0, 2), (2, 8)))
    return dict(query_rows=query_rows, key_rows=key_rows, value_rows=value_rows, residual=residual, control_mask=control_mask, step_index=step_index, step_gates=step_gates, out_weight=out_weight)


def head_attention(query_head, key_head, value_head):
    score_scale = float(DH) ** -0.5
    scores = jnp.dot(query_head, key_head.T, preferred_element_type=jnp.float32) * score_scale
    peak = jnp.max(scores, axis=1, keepdims=True)
    expo = jnp.exp(scores - peak)
    total_sum = jnp.sum(expo, axis=1, keepdims=True)
    probs = expo.astype(jnp.bfloat16)
    attended = jnp.dot(probs, value_head, preferred_element_type=jnp.float32) / total_sum
    return attended.astype(jnp.bfloat16)


def branch_projection(query_all, key_all, value_all, weight_matrix):
    query_heads = query_all.reshape(TOKENS, HEADS, DH).transpose(1, 0, 2)
    key_heads = key_all.reshape(TOKENS, HEADS, DH).transpose(1, 0, 2)
    value_heads = value_all.reshape(TOKENS, HEADS, DH).transpose(1, 0, 2)
    attended = lax.map(lambda triple: head_attention(triple[0], triple[1], triple[2]), (query_heads, key_heads, value_heads))
    attended = attended.transpose(1, 0, 2).reshape(TOKENS, HEADS * DH)
    return jnp.dot(attended, weight_matrix, preferred_element_type=jnp.float32)


def reference(query_rows, key_rows, value_rows, residual, control_mask, step_index, step_gates, out_weight):
    context_proj = branch_projection(query_rows[0], key_rows[0], value_rows[0], out_weight[0])
    main_proj = branch_projection(query_rows[1], key_rows[1], value_rows[1], out_weight[1])
    hints = jnp.where(control_mask[:, None] == 1, context_proj, jnp.zeros_like(context_proj)).astype(jnp.bfloat16)
    gate_row = lax.dynamic_slice_in_dim(step_gates, step_index[0].astype(jnp.int32), 1, 0)[0]
    mixed_out = residual.astype(jnp.float32) + gate_row[None, :] * main_proj + hints.astype(jnp.float32)
    return jnp.stack([hints, mixed_out.astype(jnp.bfloat16)])
```

```python
import math

import jax
import jax.numpy as jnp
from jax import lax
from jax.experimental import pallas as pl
from jax.experimental.pallas import tpu as pltpu
from jax.sharding import PartitionSpec as P

HEADS = 32
CHUNKS = 2


def attend_project(queries, keys_near, keys_far, values_near, values_far, weight, block_rows, head_size):
    total_rows, features = queries.shape
    count_heads = features // head_size
    near_rows = keys_near.shape[0]
    far_rows = keys_far.shape[0]
    columns = weight.shape[1]
    scale = float(head_size) ** (-0.5) * math.log2(math.e)

    def body(q_ref, kn_ref, kf_ref, vn_ref, vf_ref, w_ref, out_ref, attended):
        head = pl.program_id(1)
        query = q_ref[...]
        contract = (((1,), (1,)), ((), ()))
        near = lax.dot_general(query, kn_ref[...], contract, preferred_element_type=jnp.float32)
        far = lax.dot_general(query, kf_ref[...], contract, preferred_element_type=jnp.float32)
        peak = jnp.maximum(
            jnp.max(near, axis=1, keepdims=True), jnp.max(far, axis=1, keepdims=True)
        )
        near = jnp.exp2((near - peak) * scale)
        far = jnp.exp2((far - peak) * scale)
        total = jnp.sum(near, axis=1, keepdims=True) + jnp.sum(far, axis=1, keepdims=True)
        mixed = jnp.dot(near.astype(jnp.bfloat16), vn_ref[...], preferred_element_type=jnp.float32)
        mixed += jnp.dot(far.astype(jnp.bfloat16), vf_ref[...], preferred_element_type=jnp.float32)
        mixed = (mixed / total).astype(jnp.bfloat16)
        for index in range(count_heads):

            @pl.when(head == index)
            def _():
                attended[:, index * head_size : (index + 1) * head_size] = mixed

        @pl.when(head == count_heads - 1)
        def _():
            out_ref[...] = jnp.dot(
                attended[...], w_ref[...], preferred_element_type=jnp.float32
            ).astype(out_ref.dtype)

    def key_spec(rows):
        return pl.BlockSpec((rows, head_size), lambda block, head: (0, head))

    return pl.pallas_call(
        body,
        grid=(total_rows // block_rows, count_heads),
        in_specs=[
            pl.BlockSpec((block_rows, head_size), lambda block, head: (block, head)),
            key_spec(near_rows),
            key_spec(far_rows),
            key_spec(near_rows),
            key_spec(far_rows),
            pl.BlockSpec((features, columns), lambda block, head: (0, 0)),
        ],
        out_specs=pl.BlockSpec((block_rows, columns), lambda block, head: (block, 0)),
        out_shape=jax.ShapeDtypeStruct((total_rows, columns), jnp.bfloat16),
        scratch_shapes=[pltpu.VMEM((block_rows, features), jnp.bfloat16)],
        compiler_params=pltpu.CompilerParams(vmem_limit_bytes=48 * 1024 * 1024),
        cost_estimate=pl.CostEstimate(
            flops=4 * total_rows * (near_rows + far_rows) * features + 2 * total_rows * features * columns,
            bytes_accessed=2 * (2 * (near_rows + far_rows) * features + features * columns),
            transcendentals=total_rows * (near_rows + far_rows) * count_heads,
        ),
    )(queries, keys_near, keys_far, values_near, values_far, weight)


def per_device(
    query_rows, key_rows, value_rows, residual, control_mask, step_index, step_gates, out_weight
):
    query, key, value, weight = query_rows[0], key_rows[0], value_rows[0], out_weight[0]
    rows, all_features = query.shape
    head_size = all_features // HEADS
    count = lax.axis_size("seq")
    half = count // 2
    shares = lax.axis_size("group")
    features = all_features // half
    columns = weight.shape[1]
    branch = lax.axis_index("branch")
    group = lax.axis_index("group")
    place = lax.axis_index("seq")
    spot = place % half
    pair = ("branch", "seq")

    def crossing(step):
        return [
            (b * count + h * half + r, h * count + b * half + (r ^ step))
            for b in range(2)
            for h in range(2)
            for r in range(half)
        ]

    def sibling(array):
        return lax.ppermute(array, "branch", [(0, 1), (1, 0)])

    def scatter_columns(array):
        parts = []
        for step in range(half):
            part = lax.dynamic_slice_in_dim(array, (spot ^ step) * features, features, axis=1)
            parts.append(lax.ppermute(part, pair, crossing(step)))
        return jnp.concatenate(parts, axis=0)

    share_rows = features // shares
    parts = []
    for step in range(half):
        start = (spot ^ step) * features + group * share_rows
        part = lax.dynamic_slice_in_dim(weight, start, share_rows, axis=0)
        parts.append(lax.ppermute(part, pair, crossing(step)))
    own = jnp.stack(parts)
    blocks = own
    if shares == 2:
        other = lax.ppermute(own, "group", [(0, 1), (1, 0)])
        blocks = jnp.where(
            group == 0,
            jnp.concatenate([own, other], axis=1),
            jnp.concatenate([other, own], axis=1),
        )
    far_blocks = sibling(blocks)
    both = jnp.concatenate([blocks, far_blocks], axis=0)
    ordered = []
    for block in range(count):
        step = (block % half) ^ spot
        where = jnp.where(branch == block // half, step, half + step)
        ordered.append(lax.dynamic_index_in_dim(both, where, 0, keepdims=False))
    weight_rows = jnp.concatenate(ordered, axis=1)

    key_near = scatter_columns(key)
    key_far = sibling(key_near)
    value_near = scatter_columns(value)
    value_far = sibling(value_near)

    step_ids = lax.broadcasted_iota(jnp.int32, (step_gates.shape[0], 1), 0)
    gate_row = jnp.sum(
        jnp.where(step_ids == step_index[0], step_gates, jnp.zeros_like(step_gates)), axis=0
    )
    is_main = branch == 1
    chunk_rows = rows // CHUNKS
    outs = []
    for chunk in range(CHUNKS):
        piece = slice(chunk * chunk_rows, (chunk + 1) * chunk_rows)
        queries = scatter_columns(query[piece])
        partial = attend_project(
            queries,
            key_near,
            key_far,
            value_near,
            value_far,
            weight_rows,
            math.gcd(half, 4) * chunk_rows,
            head_size,
        ).reshape(half, chunk_rows, count * columns)
        summed = partial[0].astype(jnp.float32)
        for step in range(1, half):
            swap = [(s, s ^ step) for s in range(count)]
            summed = summed + lax.ppermute(partial[step], "seq", swap).astype(jnp.float32)
        projected = lax.ppermute(summed.astype(jnp.bfloat16), pair, crossing(0))
        hint = jnp.where(control_mask[piece, None] == 1, projected, jnp.zeros_like(projected))
        hint_moved = lax.ppermute(hint, "branch", [(0, 1)])
        mixed = (
            residual[piece].astype(jnp.float32)
            + gate_row[None, :] * projected.astype(jnp.float32)
            + hint_moved.astype(jnp.float32)
        ).astype(jnp.bfloat16)
        outs.append(jnp.where(is_main, mixed, hint))
    return jnp.concatenate(outs, axis=0)[None]


def solution(mesh):
    placed = (
        P("branch", ("group", "seq"), None),
        P("branch", ("group", "seq"), None),
        P("branch", ("group", "seq"), None),
        P(("group", "seq"), None),
        P(("group", "seq")),
        P("group"),
        P(),
        P("branch", None, "seq"),
    )
    return jax.shard_map(
        per_device,
        mesh=mesh,
        in_specs=placed,
        out_specs=P("branch", ("group", "seq"), None),
        check_vma=False,
    )
```

```python
import math

import jax
import jax.numpy as jnp
from jax import lax
from jax.experimental import pallas as pl
from jax.experimental.pallas import tpu as pltpu
from jax.sharding import PartitionSpec as P

HEADS = 32
HIDDEN = 40_000_000_000
CHUNKS = 2
JOINED = 2


def attend_project(
    query_parts, chunk_rows, context, weight_blocks, where, head_size
):
    homes, home_rows, features = context[0].shape
    home_rows = home_rows // 2
    steps = features // head_size // JOINED
    key_rows = homes * home_rows
    block_columns, share = weight_blocks[0].shape[1:]
    columns = 2 * homes * block_columns
    scale = float(head_size) ** (-0.5) * math.log2(math.e)
    together = math.gcd(homes, 4)
    block_rows = together * chunk_rows
    contract = (((1,), (1,)), ((), ()))

    def body(where, *refs):
        q_refs, refs = refs[:homes], refs[homes:]
        context_refs, weight_refs, refs = refs[:2], refs[2:6], refs[6:]
        out_refs, (attended, w_held, w_sem) = refs[:homes], refs[homes:]
        step = pl.program_id(0)
        side, mine, spot = where[0], where[1], where[2]

        def each_fetch(act):
            for index, ref in enumerate(weight_refs):
                at_side = side if index < 2 else 1 - side
                at_group = mine if index % 2 == 0 else 1 - mine
                for home in range(homes):
                    block = at_side * homes + (spot ^ home)
                    act(
                        pltpu.make_async_copy(
                            ref.at[home],
                            w_held.at[
                                pl.ds(pl.multiple_of(block * block_columns, block_columns), block_columns),
                                pl.ds(pl.multiple_of(at_group * share, share), share),
                            ],
                            w_sem.at[index, home],
                        )
                    )

        @pl.when(step == 0)
        def _():
            each_fetch(lambda copy: copy.start())

        for index in range(JOINED):
            cols = slice(index * head_size, (index + 1) * head_size)
            near_keys, far_keys, near_values, far_values = (
                ref[:, kind * home_rows : (kind + 1) * home_rows, cols].reshape(key_rows, head_size)
                for kind in range(2)
                for ref in context_refs
            )
            for first in range(0, homes, together):
                query = jnp.concatenate([ref[:, cols] for ref in q_refs[first : first + together]], axis=0)
                near = lax.dot_general(query, near_keys, contract, preferred_element_type=jnp.float32)
                far = lax.dot_general(query, far_keys, contract, preferred_element_type=jnp.float32)
                peak = jnp.maximum(
                    jnp.max(near, axis=1, keepdims=True), jnp.max(far, axis=1, keepdims=True)
                )
                near = jnp.exp2((near - peak) * scale)
                far = jnp.exp2((far - peak) * scale)
                total = jnp.sum(near, axis=1, keepdims=True) + jnp.sum(far, axis=1, keepdims=True)
                mixed = jnp.dot(near.astype(jnp.bfloat16), near_values, preferred_element_type=jnp.float32)
                mixed += jnp.dot(far.astype(jnp.bfloat16), far_values, preferred_element_type=jnp.float32)
                mixed = (mixed / total).astype(jnp.bfloat16)
                for at in range(steps):

                    @pl.when(step == at)
                    def _():
                        begin = (at * JOINED + index) * head_size
                        attended[
                            first * chunk_rows : first * chunk_rows + block_rows, begin : begin + head_size
                        ] = mixed

        @pl.when(step == steps - 1)
        def _():
            each_fetch(lambda copy: copy.wait())
            for first in range(0, homes, together):
                product = lax.dot_general(
                    attended[first * chunk_rows : first * chunk_rows + block_rows],
                    w_held[...],
                    contract,
                    preferred_element_type=jnp.float32,
                )
                for at, ref in enumerate(out_refs[first : first + together]):
                    ref[...] = product[at * chunk_rows : (at + 1) * chunk_rows].astype(ref.dtype)

    width = JOINED * head_size
    stacked = pl.BlockSpec((homes, 2 * home_rows, width), lambda step, _: (0, 0, step))
    return pl.pallas_call(
        body,
        grid_spec=pltpu.PrefetchScalarGridSpec(
            num_scalar_prefetch=1,
            grid=(steps,),
            in_specs=[
                *[pl.BlockSpec((chunk_rows, width), lambda step, _: (0, step))] * homes,
                *[stacked] * 2,
                *[pl.BlockSpec(memory_space=pl.ANY)] * 4,
            ],
            out_specs=[pl.BlockSpec((chunk_rows, columns), lambda step, _: (0, 0))] * homes,
            scratch_shapes=[
                pltpu.VMEM((homes * chunk_rows, features), jnp.bfloat16),
                pltpu.VMEM((columns, features), jnp.bfloat16),
                pltpu.SemaphoreType.DMA((4, homes)),
            ],
        ),
        out_shape=[
            jax.ShapeDtypeStruct((chunk_rows, columns), jnp.float32 if home == 0 else jnp.bfloat16)
            for home in range(homes)
        ],
        compiler_params=pltpu.CompilerParams(vmem_limit_bytes=(28 if homes <= 4 else 56) * 1024 * 1024),
        cost_estimate=pl.CostEstimate(
            flops=homes * chunk_rows * features * (8 * key_rows + 2 * columns) + 0,
            bytes_accessed=2 * features * (4 * key_rows + columns),
            transcendentals=homes * chunk_rows * 2 * key_rows * (features // head_size),
        ),
    )(where, *query_parts, *context, *weight_blocks)


def gathered(parts, rows, hidden):
    homes, width = len(parts), parts[0].shape[1]

    def body(*refs):
        part_refs, out_ref = refs[:homes], refs[homes]
        for home, ref in enumerate(part_refs):
            out_ref[home] = ref[:rows]

    return pl.pallas_call(
        body,
        out_shape=jax.ShapeDtypeStruct((homes, rows, width), parts[0].dtype),
        compiler_params=pltpu.CompilerParams(vmem_limit_bytes=16 * 1024 * 1024),
        cost_estimate=pl.CostEstimate(flops=hidden, bytes_accessed=8 * homes * rows * width, transcendentals=0),
    )(*parts)


def per_device(
    query_rows, key_rows, value_rows, residual, control_mask, step_index, step_gates, out_weight
):
    query, key, value = query_rows[0], key_rows[0], value_rows[0]
    weight = jnp.swapaxes(out_weight[0], 0, 1)
    rows, all_features = query.shape
    head_size = all_features // HEADS
    count = lax.axis_size("seq")
    half = count // 2
    shares = lax.axis_size("group")
    features = all_features // half
    columns = weight.shape[0]
    branch = lax.axis_index("branch")
    group = lax.axis_index("group")
    place = lax.axis_index("seq")
    spot = place % half
    pair = ("branch", "seq")

    def crossing(step):
        return [
            (b * count + h * half + r, h * count + b * half + (r ^ step))
            for b in range(2)
            for h in range(2)
            for r in range(half)
        ]

    def send(array, step):
        return lax.ppermute(array, pair, crossing(step))

    def sibling(array):
        return lax.ppermute(array, "branch", [(0, 1), (1, 0)])

    def after(*arrays):
        return lax.optimization_barrier(arrays)

    def mine(array, step):
        return lax.dynamic_slice_in_dim(array, (spot ^ step) * features, features, axis=-1)

    chunk_rows = rows // CHUNKS
    pieces = [slice(chunk * chunk_rows, (chunk + 1) * chunk_rows) for chunk in range(CHUNKS)]

    share = features // shares
    weight_parts = [
        send(lax.dynamic_slice_in_dim(weight, (spot ^ step) * features + group * share, share, axis=1), step)
        for step in range(half)
    ]
    own = jnp.stack(weight_parts)
    other = lax.ppermute(own, "group", [(0, 1), (1, 0)])
    where = jnp.stack([branch, group, spot]).astype(jnp.int32)
    pair_parts = []
    for step in range(half):
        part = jnp.concatenate([mine(key, step), mine(value, step)], axis=0)
        if step > 0:
            part, weight_parts[step - 1] = after(part, weight_parts[step - 1])
        pair_parts.append(send(part, step))
    own, pair_parts[0] = after(own, pair_parts[0])
    own_far, other_far = sibling(own), sibling(other)
    queries = [[mine(query[piece], step) for step in range(half)] for piece in pieces]
    for step in range(half):
        at = min(step, half - 2)
        queries[0][step], pair_parts[at] = after(queries[0][step], pair_parts[at])
    queries[0][0], own_far = after(queries[0][0], own_far)
    queries[0][2], other_far = after(queries[0][2], other_far)
    query_parts = [send(part, step) for step, part in enumerate(queries[0])]
    near = gathered(pair_parts, 2 * rows, 0)
    far = sibling(near)
    queries[1][0], far = after(queries[1][0], far)
    query_parts = [query_parts, [send(part, step) for step, part in enumerate(queries[1])]]
    weight_blocks = (own, other, own_far, other_far)

    partials = [
        attend_project(
            parts,
            chunk_rows,
            (near, far),
            weight_blocks,
            where,
            head_size,
        )
        for parts in query_parts
    ]

    step_ids = lax.broadcasted_iota(jnp.int32, (step_gates.shape[0], 1), 0)
    gate_row = jnp.sum(
        jnp.where(step_ids == step_index[0], step_gates, jnp.zeros_like(step_gates)), axis=0
    )
    is_main = branch == 1
    outs = []
    for piece, partial in zip(pieces, partials):
        summed = partial[0]
        for step in range(1, half):
            swap = [(s, s ^ step) for s in range(count)]
            summed = summed + lax.ppermute(partial[step], "seq", swap).astype(jnp.float32)
        projected = send(summed.astype(jnp.bfloat16), 0)
        hint = jnp.where(control_mask[piece, None] == 1, projected, jnp.zeros_like(projected))
        hint_moved = lax.ppermute(hint, "branch", [(0, 1)])
        mixed = (
            residual[piece].astype(jnp.float32)
            + gate_row[None, :] * projected.astype(jnp.float32)
            + hint_moved.astype(jnp.float32)
        ).astype(jnp.bfloat16)
        outs.append(jnp.where(is_main, mixed, hint))
    return jnp.concatenate(outs, axis=0)[None]


def solution(mesh):
    placed = (
        P("branch", ("group", "seq"), None),
        P("branch", ("group", "seq"), None),
        P("branch", ("group", "seq"), None),
        P(("group", "seq"), None),
        P(("group", "seq")),
        P("group"),
        P(),
        P("branch", None, "seq"),
    )
    return jax.shard_map(
        per_device,
        mesh=mesh,
        in_specs=placed,
        out_specs=P("branch", ("group", "seq"), None),
        check_vma=False,
    )
```

```python
import math

import jax
import jax.numpy as jnp
from jax import lax
from jax.experimental import pallas as pl
from jax.experimental.pallas import tpu as pltpu
from jax.sharding import PartitionSpec as P

HEADS = 32
CHUNKS = (1, 1)
JOINED = 4


def attend_project(
    query_parts, context, weight_blocks, where, head_size
):
    homes, home_rows, features = context[0].shape
    home_rows = home_rows // 2
    chunk_rows = query_parts[0].shape[0]
    joined = math.gcd(features // head_size, JOINED)
    steps = features // head_size // joined
    key_rows = homes * home_rows
    block_columns, share = weight_blocks[0].shape[1:]
    columns = 2 * homes * block_columns
    scale = float(head_size) ** (-0.5) * math.log2(math.e)
    together = math.gcd(homes, 4)
    block_rows = together * chunk_rows
    contract = (((1,), (1,)), ((), ()))

    def body(where, *refs):
        q_refs, refs = refs[:homes], refs[homes:]
        context_refs, weight_refs, refs = refs[:2], refs[2:6], refs[6:]
        out_refs, (attended, w_held, w_sem) = refs[:homes], refs[homes:]
        step = pl.program_id(0)
        side, mine, spot = where[0], where[1], where[2]

        def each_fetch(act):
            for index, ref in enumerate(weight_refs):
                at_side = side if index < 2 else 1 - side
                at_group = mine if index % 2 == 0 else 1 - mine
                for home in range(homes):
                    block = at_side * homes + (spot ^ home)
                    act(
                        pltpu.make_async_copy(
                            ref.at[home],
                            w_held.at[
                                pl.ds(pl.multiple_of(block * block_columns, block_columns), block_columns),
                                pl.ds(pl.multiple_of(at_group * share, share), share),
                            ],
                            w_sem.at[index, home],
                        )
                    )

        @pl.when(step == 0)
        def _():
            each_fetch(lambda copy: copy.start())

        def columns_of(index):
            return slice(index * head_size, (index + 1) * head_size)

        def held(kind, index):
            return [
                ref[:, kind * home_rows : (kind + 1) * home_rows, columns_of(index)].reshape(key_rows, head_size)
                for ref in context_refs
            ]

        def scored(first, index):
            query = jnp.concatenate([ref[:, columns_of(index)] for ref in q_refs[first : first + together]], axis=0)
            return [
                lax.dot_general(query, keys, contract, preferred_element_type=jnp.float32)
                for keys in held(0, index)
            ]

        def weighed(scores):
            peaks = [jnp.max(score, axis=1, keepdims=True) for score in scores]
            peak = jnp.maximum(*peaks)
            expo = [jnp.exp2((score - peak) * scale) for score in scores]
            total = sum(jnp.sum(part, axis=1, keepdims=True) for part in expo)
            return [part.astype(jnp.bfloat16) for part in expo], total

        def mix(first, index, probs, total):
            near, far = (
                jnp.dot(prob, values, preferred_element_type=jnp.float32)
                for prob, values in zip(probs, held(1, index))
            )
            mixed = ((near + far) / total).astype(jnp.bfloat16)
            for at in range(steps):

                @pl.when(step == at)
                def _():
                    begin = (at * joined + index) * head_size
                    attended[first * chunk_rows : first * chunk_rows + block_rows, begin : begin + head_size] = mixed

        work = [(first, index) for first in range(0, homes, together) for index in range(joined)]
        scores = scored(*work[0])
        waiting = None
        for position, item in enumerate(work):
            ahead = scored(*work[position + 1]) if position + 1 < len(work) else None
            current = weighed(scores)
            if waiting is not None:
                mix(*work[position - 1], *waiting)
            scores, waiting = ahead, current
        mix(*work[-1], *waiting)

        @pl.when(step == steps - 1)
        def _():
            each_fetch(lambda copy: copy.wait())
            for first in range(0, homes, together):
                product = lax.dot_general(
                    attended[first * chunk_rows : first * chunk_rows + block_rows],
                    w_held[...],
                    contract,
                    preferred_element_type=jnp.float32,
                )
                for at, ref in enumerate(out_refs[first : first + together]):
                    ref[...] = product[at * chunk_rows : (at + 1) * chunk_rows].astype(ref.dtype)

    width = joined * head_size
    stacked = pl.BlockSpec((homes, 2 * home_rows, width), lambda step, _: (0, 0, step))
    return pl.pallas_call(
        body,
        grid_spec=pltpu.PrefetchScalarGridSpec(
            num_scalar_prefetch=1,
            grid=(steps,),
            in_specs=[
                *[pl.BlockSpec((chunk_rows, width), lambda step, _: (0, step))] * homes,
                *[stacked] * 2,
                *[pl.BlockSpec(memory_space=pl.ANY)] * 4,
            ],
            out_specs=[pl.BlockSpec((chunk_rows, columns), lambda step, _: (0, 0))] * homes,
            scratch_shapes=[
                pltpu.VMEM((homes * chunk_rows, features), jnp.bfloat16),
                pltpu.VMEM((columns, features), jnp.bfloat16),
                pltpu.SemaphoreType.DMA((4, homes)),
            ],
        ),
        out_shape=[
            jax.ShapeDtypeStruct((chunk_rows, columns), jnp.float32 if home == 0 else jnp.bfloat16)
            for home in range(homes)
        ],
        compiler_params=pltpu.CompilerParams(vmem_limit_bytes=(28 if homes <= 4 else 56) * 1024 * 1024),
        cost_estimate=pl.CostEstimate(
            flops=homes * chunk_rows * features * (8 * key_rows + 2 * columns) + 0,
            bytes_accessed=2 * features * (4 * key_rows + columns),
            transcendentals=homes * chunk_rows * 2 * key_rows * (features // head_size),
        ),
    )(where, *query_parts, *context, *weight_blocks)


def gathered(parts, rows, hidden):
    homes, width = len(parts), parts[0].shape[1]

    def body(*refs):
        part_refs, out_ref = refs[:homes], refs[homes]
        for home, ref in enumerate(part_refs):
            out_ref[home] = ref[:rows]

    return pl.pallas_call(
        body,
        out_shape=jax.ShapeDtypeStruct((homes, rows, width), parts[0].dtype),
        compiler_params=pltpu.CompilerParams(vmem_limit_bytes=16 * 1024 * 1024),
        cost_estimate=pl.CostEstimate(flops=hidden, bytes_accessed=8 * homes * rows * width, transcendentals=0),
    )(*parts)


def per_device(
    query_rows, key_rows, value_rows, residual, control_mask, step_index, step_gates, out_weight
):
    query, key, value = query_rows[0], key_rows[0], value_rows[0]
    weight = jnp.swapaxes(out_weight[0], 0, 1)
    rows, all_features = query.shape
    head_size = all_features // HEADS
    count = lax.axis_size("seq")
    half = count // 2
    shares = lax.axis_size("group")
    features = all_features // half
    columns = weight.shape[0]
    branch = lax.axis_index("branch")
    group = lax.axis_index("group")
    place = lax.axis_index("seq")
    spot = place % half
    pair = ("branch", "seq")

    def crossing(step):
        return [
            (b * count + h * half + r, h * count + b * half + (r ^ step))
            for b in range(2)
            for h in range(2)
            for r in range(half)
        ]

    def send(array, step):
        return lax.ppermute(array, pair, crossing(step))

    def sibling(array):
        return lax.ppermute(array, "branch", [(0, 1), (1, 0)])

    def after(*arrays):
        return lax.optimization_barrier(arrays)

    def mine(array, step):
        return lax.dynamic_slice_in_dim(array, (spot ^ step) * features, features, axis=-1)

    ends = [rows * sum(CHUNKS[: chunk + 1]) // sum(CHUNKS) for chunk in range(len(CHUNKS))]
    pieces = [slice(first, last) for first, last in zip([0, *ends], ends)]

    share = features // shares
    weight_parts = [
        send(lax.dynamic_slice_in_dim(weight, (spot ^ step) * features + group * share, share, axis=1), step)
        for step in range(half)
    ]
    own = jnp.stack(weight_parts)
    other = lax.ppermute(own, "group", [(0, 1), (1, 0)])
    where = jnp.stack([branch, group, spot]).astype(jnp.int32)
    pair_parts = []
    for step in range(half):
        part = jnp.concatenate([mine(key, step), mine(value, step)], axis=0)
        if step > 0:
            part, weight_parts[step - 1] = after(part, weight_parts[step - 1])
        pair_parts.append(send(part, step))
    own, pair_parts[0] = after(own, pair_parts[0])
    own_far, other_far = sibling(own), sibling(other)
    queries = [[mine(query[piece], step) for step in range(half)] for piece in pieces]
    for step in range(half):
        at = min(step, half - 2)
        queries[0][step], pair_parts[at] = after(queries[0][step], pair_parts[at])
    queries[0][2], own_far = after(queries[0][2], own_far)
    query_parts = [send(part, step) for step, part in enumerate(queries[0])]
    near = gathered(pair_parts, 2 * rows, 0)
    far = sibling(near)
    queries[1][0], other_far = after(queries[1][0], other_far)
    queries[1][0], far = after(queries[1][0], far)
    query_parts = [query_parts] + [
        [send(part, step) for step, part in enumerate(parts)] for parts in queries[1:]
    ]
    weight_blocks = (own, other, own_far, other_far)

    partials = [
        attend_project(
            parts,
            (near, far),
            weight_blocks,
            where,
            head_size,
        )
        for parts in query_parts
    ]

    step_ids = lax.broadcasted_iota(jnp.int32, (step_gates.shape[0], 1), 0)
    gate_row = jnp.sum(
        jnp.where(step_ids == step_index[0], step_gates, jnp.zeros_like(step_gates)), axis=0
    )
    is_main = branch == 1
    wanted = control_mask[:, None] == 1
    result = jnp.zeros_like(residual)
    for piece, partial in zip(pieces, partials):
        summed = partial[0]
        for step in range(1, half):
            swap = [(s, s ^ step) for s in range(count)]
            summed = summed + lax.ppermute(partial[step], "seq", swap).astype(jnp.float32)
        projected = send(summed.astype(jnp.bfloat16), 0)
        context_rows = jnp.where(is_main, lax.ppermute(projected, "branch", [(0, 1)]), projected)
        hint = jnp.where(wanted[piece], context_rows, jnp.zeros_like(projected))
        mixed = (
            residual[piece].astype(jnp.float32)
            + gate_row[None, :] * projected.astype(jnp.float32)
            + hint.astype(jnp.float32)
        ).astype(jnp.bfloat16)
        result = lax.dynamic_update_slice(result, jnp.where(is_main, mixed, hint), (piece.start, 0))
    return result[None]


def solution(mesh):
    placed = (
        P("branch", ("group", "seq"), None),
        P("branch", ("group", "seq"), None),
        P("branch", ("group", "seq"), None),
        P(("group", "seq"), None),
        P(("group", "seq")),
        P("group"),
        P(),
        P("branch", None, "seq"),
    )
    return jax.shard_map(
        per_device,
        mesh=mesh,
        in_specs=placed,
        out_specs=P("branch", ("group", "seq"), None),
        check_vma=False,
    )
```

```python
import math

import jax
import jax.numpy as jnp
from jax import lax
from jax.experimental import pallas as pl
from jax.experimental.pallas import tpu as pltpu
from jax.sharding import PartitionSpec as P

HEADS = 32
CHUNKS = (4, 6)
ROWS_SENT = ((1,), (3, 3))
JOINED = 4


def attend_project(
    query_parts, marks, context, weight_blocks, where, head_size
):
    homes, home_rows, features = context[0].shape
    home_rows = home_rows // 2
    chunk_rows = query_parts[0].shape[0]
    groups = len(marks) - 1
    joined = math.gcd(features // head_size, JOINED)
    steps = features // head_size // joined
    key_rows = homes * home_rows
    block_columns, share = weight_blocks[0].shape[1:]
    columns = 2 * homes * block_columns
    scale = float(head_size) ** (-0.5) * math.log2(math.e)
    together = math.gcd(homes, 4)
    block_rows = together * chunk_rows
    contract = (((1,), (1,)), ((), ()))

    def body(where, *refs):
        q_refs, refs = refs[:homes], refs[homes:]
        context_refs, weight_refs, refs = refs[:2], refs[2:6], refs[6:]
        out_refs, (attended, w_held, w_sem) = refs[: homes * groups], refs[homes * groups :]
        step = pl.program_id(0)
        side, mine, spot = where[0], where[1], where[2]

        def each_fetch(act):
            for index, ref in enumerate(weight_refs):
                at_side = side if index < 2 else 1 - side
                at_group = mine if index % 2 == 0 else 1 - mine
                for home in range(homes):
                    block = at_side * homes + (spot ^ home)
                    act(
                        pltpu.make_async_copy(
                            ref.at[home],
                            w_held.at[
                                pl.ds(pl.multiple_of(block * block_columns, block_columns), block_columns),
                                pl.ds(pl.multiple_of(at_group * share, share), share),
                            ],
                            w_sem.at[index, home],
                        )
                    )

        @pl.when(step == 0)
        def _():
            each_fetch(lambda copy: copy.start())

        def columns_of(index):
            return slice(index * head_size, (index + 1) * head_size)

        def held(kind, index):
            return [
                ref[:, kind * home_rows : (kind + 1) * home_rows, columns_of(index)].reshape(key_rows, head_size)
                for ref in context_refs
            ]

        def scored(first, index):
            query = jnp.concatenate([ref[:, columns_of(index)] for ref in q_refs[first : first + together]], axis=0)
            return [
                lax.dot_general(query, keys, contract, preferred_element_type=jnp.float32)
                for keys in held(0, index)
            ]

        def weighed(scores):
            peaks = [jnp.max(score, axis=1, keepdims=True) for score in scores]
            peak = jnp.maximum(*peaks)
            expo = [jnp.exp2((score - peak) * scale) for score in scores]
            total = sum(jnp.sum(part, axis=1, keepdims=True) for part in expo)
            return [part.astype(jnp.bfloat16) for part in expo], total

        def mix(first, index, probs, total):
            near, far = (
                jnp.dot(prob, values, preferred_element_type=jnp.float32)
                for prob, values in zip(probs, held(1, index))
            )
            mixed = ((near + far) / total).astype(jnp.bfloat16)
            for at in range(steps):

                @pl.when(step == at)
                def _():
                    begin = (at * joined + index) * head_size
                    attended[first * chunk_rows : first * chunk_rows + block_rows, begin : begin + head_size] = mixed

        work = [(first, index) for first in range(0, homes, together) for index in range(joined)]
        scores = scored(*work[0])
        waiting = None
        for position, item in enumerate(work):
            ahead = scored(*work[position + 1]) if position + 1 < len(work) else None
            current = weighed(scores)
            if waiting is not None:
                mix(*work[position - 1], *waiting)
            scores, waiting = ahead, current
        mix(*work[-1], *waiting)

        @pl.when(step == steps - 1)
        def _():
            each_fetch(lambda copy: copy.wait())
            for first in range(0, homes, together):
                product = lax.dot_general(
                    attended[first * chunk_rows : first * chunk_rows + block_rows],
                    w_held[...],
                    contract,
                    preferred_element_type=jnp.float32,
                )
                for at in range(together):
                    for some in range(groups):
                        ref = out_refs[some * homes + first + at]
                        begin, end = (at * chunk_rows + mark for mark in marks[some : some + 2])
                        ref[...] = product[begin:end].astype(ref.dtype)

    width = joined * head_size
    stacked = pl.BlockSpec((homes, 2 * home_rows, width), lambda step, _: (0, 0, step))
    return pl.pallas_call(
        body,
        grid_spec=pltpu.PrefetchScalarGridSpec(
            num_scalar_prefetch=1,
            grid=(steps,),
            in_specs=[
                *[pl.BlockSpec((chunk_rows, width), lambda step, _: (0, step))] * homes,
                *[stacked] * 2,
                *[pl.BlockSpec(memory_space=pl.ANY)] * 4,
            ],
            out_specs=[
                pl.BlockSpec((last - first, columns), lambda step, _: (0, 0))
                for first, last in zip(marks, marks[1:])
                for home in range(homes)
            ],
            scratch_shapes=[
                pltpu.VMEM((homes * chunk_rows, features), jnp.bfloat16),
                pltpu.VMEM((columns, features), jnp.bfloat16),
                pltpu.SemaphoreType.DMA((4, homes)),
            ],
        ),
        out_shape=[
            jax.ShapeDtypeStruct((last - first, columns), jnp.float32 if home == 0 else jnp.bfloat16)
            for first, last in zip(marks, marks[1:])
            for home in range(homes)
        ],
        compiler_params=pltpu.CompilerParams(vmem_limit_bytes=(28 if homes <= 4 else 56) * 1024 * 1024),
        cost_estimate=pl.CostEstimate(
            flops=homes * chunk_rows * features * (8 * key_rows + 2 * columns),
            bytes_accessed=2 * features * (4 * key_rows + columns),
            transcendentals=homes * chunk_rows * 2 * key_rows * (features // head_size),
        ),
    )(where, *query_parts, *context, *weight_blocks)


def gathered(parts, rows):
    homes, width = len(parts), parts[0].shape[1]

    def body(*refs):
        part_refs, out_ref = refs[:homes], refs[homes]
        for home, ref in enumerate(part_refs):
            out_ref[home] = ref[:rows]

    return pl.pallas_call(
        body,
        out_shape=jax.ShapeDtypeStruct((homes, rows, width), parts[0].dtype),
        compiler_params=pltpu.CompilerParams(vmem_limit_bytes=16 * 1024 * 1024),
        cost_estimate=pl.CostEstimate(flops=0, bytes_accessed=8 * homes * rows * width, transcendentals=0),
    )(*parts)


def per_device(
    query_rows, key_rows, value_rows, residual, control_mask, step_index, step_gates, out_weight
):
    query, key, value = query_rows[0], key_rows[0], value_rows[0]
    weight = jnp.swapaxes(out_weight[0], 0, 1)
    rows, all_features = query.shape
    head_size = all_features // HEADS
    count = lax.axis_size("seq")
    half = count // 2
    shares = lax.axis_size("group")
    features = all_features // half
    columns = weight.shape[0]
    branch = lax.axis_index("branch")
    group = lax.axis_index("group")
    place = lax.axis_index("seq")
    spot = place % half
    pair = ("branch", "seq")

    def crossing(step):
        return [
            (b * count + h * half + r, h * count + b * half + (r ^ step))
            for b in range(2)
            for h in range(2)
            for r in range(half)
        ]

    def send(array, step):
        return lax.ppermute(array, pair, crossing(step))

    def sibling(array):
        return lax.ppermute(array, "branch", [(0, 1), (1, 0)])

    def after(*arrays):
        return lax.optimization_barrier(arrays)

    def mine(array, step):
        return lax.dynamic_slice_in_dim(array, (spot ^ step) * features, features, axis=-1)

    ends = [rows * sum(CHUNKS[: chunk + 1]) // sum(CHUNKS) for chunk in range(len(CHUNKS))]
    pieces = [slice(first, last) for first, last in zip([0, *ends], ends)]

    share = features // shares
    weight_parts = [
        send(lax.dynamic_slice_in_dim(weight, (spot ^ step) * features + group * share, share, axis=1), step)
        for step in range(half)
    ]
    own = jnp.stack(weight_parts)
    other = lax.ppermute(own, "group", [(0, 1), (1, 0)])
    where = jnp.stack([branch, group, spot]).astype(jnp.int32)
    pair_parts = []
    for step in range(half):
        part = jnp.concatenate([mine(key, step), mine(value, step)], axis=0)
        if step > 0:
            part, weight_parts[step - 1] = after(part, weight_parts[step - 1])
        if step == half - 1:
            part, weight_parts[step] = after(part, weight_parts[step])
        pair_parts.append(send(part, step))
    own, pair_parts[0] = after(own, pair_parts[0])
    own_far, other_far = sibling(own), sibling(other)
    queries = [[mine(query[piece], step) for step in range(half)] for piece in pieces]
    for step in range(half):
        at = min(step, half - 2)
        queries[0][step], pair_parts[at] = after(queries[0][step], pair_parts[at])
    queries[0][2], own_far = after(queries[0][2], own_far)
    query_parts = [send(part, step) for step, part in enumerate(queries[0])]
    near = gathered(pair_parts, 2 * rows)
    far = sibling(near)
    queries[1][3], other_far = after(queries[1][3], other_far)
    queries[1][3], far = after(queries[1][3], far)
    query_parts = [query_parts] + [
        [send(part, step) for step, part in enumerate(parts)] for parts in queries[1:]
    ]
    weight_blocks = (own, other, own_far, other_far)

    partials, done_rows = [], []
    for parts, piece, sizes in zip(query_parts, pieces, ROWS_SENT):
        length = piece.stop - piece.start
        marks = [length * sum(sizes[:at]) // sum(sizes) for at in range(len(sizes) + 1)]
        if partials:
            parts[0], partials[-1][0] = after(parts[0], partials[-1][0])
        sums = attend_project(parts, marks, (near, far), weight_blocks, where, head_size)
        for at in range(len(sizes)):
            partials.append(list(sums[at * half : (at + 1) * half]))
            done_rows.append(slice(piece.start + marks[at], piece.start + marks[at + 1]))

    step_ids = lax.broadcasted_iota(jnp.int32, (step_gates.shape[0], 1), 0)
    gate_row = jnp.sum(
        jnp.where(step_ids == step_index[0], step_gates, jnp.zeros_like(step_gates)), axis=0
    )
    is_main = branch == 1
    wanted = control_mask[:, None] == 1
    result = jnp.zeros_like(residual)
    arrived = []
    for piece, partial in zip(done_rows, partials):
        parts = []
        for step in range(1, half):
            part = partial[step]
            if len(arrived) >= 2:
                part, arrived[0][step - 1] = after(part, arrived[0][step - 1])
            swap = [(s, s ^ step) for s in range(count)]
            parts.append(lax.ppermute(part, "seq", swap))
        arrived.append(parts)
    for piece, partial, parts in zip(done_rows, partials, arrived):
        summed = partial[0]
        for part in parts:
            summed = summed + part.astype(jnp.float32)
        projected = send(summed.astype(jnp.bfloat16), 0)
        context_rows = jnp.where(is_main, lax.ppermute(projected, "branch", [(0, 1)]), projected)
        hint = jnp.where(wanted[piece], context_rows, jnp.zeros_like(projected))
        mixed = (
            residual[piece].astype(jnp.float32)
            + gate_row[None, :] * projected.astype(jnp.float32)
            + hint.astype(jnp.float32)
        ).astype(jnp.bfloat16)
        result = lax.dynamic_update_slice(result, jnp.where(is_main, mixed, hint), (piece.start, 0))
    return result[None]


def solution(mesh):
    placed = (
        P("branch", ("group", "seq"), None),
        P("branch", ("group", "seq"), None),
        P("branch", ("group", "seq"), None),
        P(("group", "seq"), None),
        P(("group", "seq")),
        P("group"),
        P(),
        P("branch", None, "seq"),
    )
    return jax.shard_map(
        per_device,
        mesh=mesh,
        in_specs=placed,
        out_specs=P("branch", ("group", "seq"), None),
        check_vma=False,
    )
```

```python
import math

import jax
import jax.numpy as jnp
from jax import lax
from jax.experimental import pallas as pl
from jax.experimental.pallas import tpu as pltpu
from jax.sharding import PartitionSpec as P

HEADS = 32
CHUNKS = (4, 6)
ROWS_SENT = ((1,), (3, 3))
JOINED = 4


def attend_project(
    query_parts, marks, context, weight_blocks, where, head_size
):
    homes, home_rows, features = context[0].shape
    home_rows = home_rows // 2
    chunk_rows = query_parts[0].shape[0]
    groups = len(marks) - 1
    joined = math.gcd(features // head_size, JOINED)
    steps = features // head_size // joined
    key_rows = homes * home_rows
    block_columns, share = weight_blocks[0].shape[1:]
    columns = 2 * homes * block_columns
    scale = float(head_size) ** (-0.5) * math.log2(math.e)
    together = math.gcd(homes, 4)
    block_rows = together * chunk_rows
    contract = (((1,), (1,)), ((), ()))

    def body(where, *refs):
        q_refs, refs = refs[:homes], refs[homes:]
        context_refs, weight_refs, refs = refs[:2], refs[2:6], refs[6:]
        out_refs, (attended, w_held, w_sem) = refs[: homes * groups], refs[homes * groups :]
        step = pl.program_id(0)
        side, mine, spot = where[0], where[1], where[2]

        def each_fetch(act):
            for index, ref in enumerate(weight_refs):
                at_side = side if index < 2 else 1 - side
                at_group = mine if index % 2 == 0 else 1 - mine
                for home in range(homes):
                    block = at_side * homes + (spot ^ home)
                    act(
                        pltpu.make_async_copy(
                            ref.at[home],
                            w_held.at[
                                pl.ds(pl.multiple_of(block * block_columns, block_columns), block_columns),
                                pl.ds(pl.multiple_of(at_group * share, share), share),
                            ],
                            w_sem.at[index, home],
                        )
                    )

        @pl.when(step == 0)
        def _():
            each_fetch(lambda copy: copy.start())

        def columns_of(index):
            return slice(index * head_size, (index + 1) * head_size)

        def held(kind, index):
            return [
                ref[:, kind * home_rows : (kind + 1) * home_rows, columns_of(index)].reshape(key_rows, head_size)
                for ref in context_refs
            ]

        def scored(first, index):
            query = jnp.concatenate([ref[:, columns_of(index)] for ref in q_refs[first : first + together]], axis=0)
            return [
                lax.dot_general(query, keys, contract, preferred_element_type=jnp.float32)
                for keys in held(0, index)
            ]

        def weighed(scores):
            peaks = [jnp.max(score, axis=1, keepdims=True) for score in scores]
            peak = jnp.maximum(*peaks)
            expo = [jnp.exp2((score - peak) * scale) for score in scores]
            total = sum(jnp.sum(part, axis=1, keepdims=True) for part in expo)
            return [part.astype(jnp.bfloat16) for part in expo], total

        def mix(first, index, probs, total):
            near, far = (
                jnp.dot(prob, values, preferred_element_type=jnp.float32)
                for prob, values in zip(probs, held(1, index))
            )
            mixed = ((near + far) / total).astype(jnp.bfloat16)
            for at in range(steps):

                @pl.when(step == at)
                def _():
                    begin = (at * joined + index) * head_size
                    attended[first * chunk_rows : first * chunk_rows + block_rows, begin : begin + head_size] = mixed

        work = [(first, index) for first in range(0, homes, together) for index in range(joined)]
        scores = scored(*work[0])
        waiting = None
        for position, item in enumerate(work):
            ahead = scored(*work[position + 1]) if position + 1 < len(work) else None
            current = weighed(scores)
            if waiting is not None:
                mix(*work[position - 1], *waiting)
            scores, waiting = ahead, current
        mix(*work[-1], *waiting)

        @pl.when(step == steps - 1)
        def _():
            each_fetch(lambda copy: copy.wait())
            for first in range(0, homes, together):
                product = lax.dot_general(
                    attended[first * chunk_rows : first * chunk_rows + block_rows],
                    w_held[...],
                    contract,
                    preferred_element_type=jnp.float32,
                )
                for at in range(together):
                    for some in range(groups):
                        ref = out_refs[some * homes + first + at]
                        begin, end = (at * chunk_rows + mark for mark in marks[some : some + 2])
                        ref[...] = product[begin:end].astype(ref.dtype)

    width = joined * head_size
    stacked = pl.BlockSpec((homes, 2 * home_rows, width), lambda step, _: (0, 0, step))
    return pl.pallas_call(
        body,
        grid_spec=pltpu.PrefetchScalarGridSpec(
            num_scalar_prefetch=1,
            grid=(steps,),
            in_specs=[
                *[pl.BlockSpec((chunk_rows, width), lambda step, _: (0, step))] * homes,
                *[stacked] * 2,
                *[pl.BlockSpec(memory_space=pl.ANY)] * 4,
            ],
            out_specs=[
                pl.BlockSpec((last - first, columns), lambda step, _: (0, 0))
                for first, last in zip(marks, marks[1:])
                for home in range(homes)
            ],
            scratch_shapes=[
                pltpu.VMEM((homes * chunk_rows, features), jnp.bfloat16),
                pltpu.VMEM((columns, features), jnp.bfloat16),
                pltpu.SemaphoreType.DMA((4, homes)),
            ],
        ),
        out_shape=[
            jax.ShapeDtypeStruct((last - first, columns), jnp.float32 if home == 0 else jnp.bfloat16)
            for first, last in zip(marks, marks[1:])
            for home in range(homes)
        ],
        compiler_params=pltpu.CompilerParams(vmem_limit_bytes=(28 if homes <= 4 else 56) * 1024 * 1024),
        cost_estimate=pl.CostEstimate(
            flops=homes * chunk_rows * features * (8 * key_rows + 2 * columns),
            bytes_accessed=2 * features * (4 * key_rows + columns),
            transcendentals=homes * chunk_rows * 2 * key_rows * (features // head_size),
        ),
    )(where, *query_parts, *context, *weight_blocks)


def gathered(parts, rows):
    homes, width = len(parts), parts[0].shape[1]

    def body(*refs):
        part_refs, out_ref = refs[:homes], refs[homes]
        for home, ref in enumerate(part_refs):
            out_ref[home] = ref[:rows]

    return pl.pallas_call(
        body,
        out_shape=jax.ShapeDtypeStruct((homes, rows, width), parts[0].dtype),
        compiler_params=pltpu.CompilerParams(vmem_limit_bytes=16 * 1024 * 1024),
        cost_estimate=pl.CostEstimate(flops=0, bytes_accessed=8 * homes * rows * width, transcendentals=0),
    )(*parts)


def per_device(
    query_rows, key_rows, value_rows, residual, control_mask, step_index, step_gates, out_weight
):
    query, key, value = query_rows[0], key_rows[0], value_rows[0]
    weight = jnp.swapaxes(out_weight[0], 0, 1)
    rows, all_features = query.shape
    head_size = all_features // HEADS
    count = lax.axis_size("seq")
    half = count // 2
    shares = lax.axis_size("group")
    features = all_features // half
    columns = weight.shape[0]
    branch = lax.axis_index("branch")
    group = lax.axis_index("group")
    place = lax.axis_index("seq")
    spot = place % half
    pair = ("branch", "seq")

    def crossing(step):
        return [
            (b * count + h * half + r, h * count + b * half + (r ^ step))
            for b in range(2)
            for h in range(2)
            for r in range(half)
        ]

    def send(array, step):
        return lax.ppermute(array, pair, crossing(step))

    def sibling(array):
        return lax.ppermute(array, "branch", [(0, 1), (1, 0)])

    def after(*arrays):
        return lax.optimization_barrier(arrays)

    def mine(array, step):
        return lax.dynamic_slice_in_dim(array, (spot ^ step) * features, features, axis=-1)

    ends = [rows * sum(CHUNKS[: chunk + 1]) // sum(CHUNKS) for chunk in range(len(CHUNKS))]
    pieces = [slice(first, last) for first, last in zip([0, *ends], ends)]

    share = features // shares
    weight_parts = [
        send(lax.dynamic_slice_in_dim(weight, (spot ^ step) * features + group * share, share, axis=1), step)
        for step in range(half)
    ]
    own = jnp.stack(weight_parts)
    other = lax.ppermute(own, "group", [(0, 1), (1, 0)])
    where = jnp.stack([branch, group, spot]).astype(jnp.int32)
    pair_parts = []
    for step in range(half):
        part = jnp.concatenate([mine(key, step), mine(value, step)], axis=0)
        if step > 0:
            part, weight_parts[step - 1] = after(part, weight_parts[step - 1])
        if step == half - 2:
            part, weight_parts[step + 1] = after(part, weight_parts[step + 1])
        pair_parts.append(send(part, step))
    own, pair_parts[0] = after(own, pair_parts[0])
    own_far, other_far = sibling(own), sibling(other)
    queries = [[mine(query[piece], step) for step in range(half)] for piece in pieces]
    for step in range(half):
        at = min(step, half - 2)
        queries[0][step], pair_parts[at] = after(queries[0][step], pair_parts[at])
    queries[0][2], own_far = after(queries[0][2], own_far)
    query_parts = [send(part, step) for step, part in enumerate(queries[0])]
    near = gathered(pair_parts, 2 * rows)
    far = sibling(near)
    queries[1][3], other_far = after(queries[1][3], other_far)
    queries[1][3], far = after(queries[1][3], far)
    query_parts = [query_parts] + [
        [send(part, step) for step, part in enumerate(parts)] for parts in queries[1:]
    ]
    weight_blocks = (own, other, own_far, other_far)

    partials, done_rows = [], []
    for parts, piece, sizes in zip(query_parts, pieces, ROWS_SENT):
        length = piece.stop - piece.start
        marks = [length * sum(sizes[:at]) // sum(sizes) for at in range(len(sizes) + 1)]
        if partials:
            parts[0], partials[-1][0] = after(parts[0], partials[-1][0])
        sums = attend_project(parts, marks, (near, far), weight_blocks, where, head_size)
        for at in range(len(sizes)):
            partials.append(list(sums[at * half : (at + 1) * half]))
            done_rows.append(slice(piece.start + marks[at], piece.start + marks[at + 1]))

    step_ids = lax.broadcasted_iota(jnp.int32, (step_gates.shape[0], 1), 0)
    gate_row = jnp.sum(
        jnp.where(step_ids == step_index[0], step_gates, jnp.zeros_like(step_gates)), axis=0
    )
    is_main = branch == 1
    wanted = control_mask[:, None] == 1
    result = jnp.zeros_like(residual)
    arrived = []
    for piece, partial in zip(done_rows, partials):
        parts = []
        for step in range(1, half):
            part = partial[step]
            if len(arrived) >= 2:
                part, arrived[0][step - 1] = after(part, arrived[0][step - 1])
            swap = [(s, s ^ step) for s in range(count)]
            parts.append(lax.ppermute(part, "seq", swap))
        arrived.append(parts)
    for piece, partial, parts in zip(done_rows, partials, arrived):
        summed = partial[0]
        for part in parts:
            summed = summed + part.astype(jnp.float32)
        projected = send(summed.astype(jnp.bfloat16), 0)
        context_rows = jnp.where(is_main, lax.ppermute(projected, "branch", [(0, 1)]), projected)
        hint = jnp.where(wanted[piece], context_rows, jnp.zeros_like(projected))
        mixed = (
            residual[piece].astype(jnp.float32)
            + gate_row[None, :] * projected.astype(jnp.float32)
            + hint.astype(jnp.float32)
        ).astype(jnp.bfloat16)
        result = lax.dynamic_update_slice(result, jnp.where(is_main, mixed, hint), (piece.start, 0))
    return result[None]


def solution(mesh):
    placed = (
        P("branch", ("group", "seq"), None),
        P("branch", ("group", "seq"), None),
        P("branch", ("group", "seq"), None),
        P(("group", "seq"), None),
        P(("group", "seq")),
        P("group"),
        P(),
        P("branch", None, "seq"),
    )
    return jax.shard_map(
        per_device,
        mesh=mesh,
        in_specs=placed,
        out_specs=P("branch", ("group", "seq"), None),
        check_vma=False,
    )
```
